32 devices in a mesh: group: 8 (over z, y), chain: 4 (over x, core).
Axes of the slice: x: 2, y: 2, z: 4, core: 2. Of those that a mesh axis runs over, the one named last changes fastest.
Arguments:
- query_gates: bfloat16 [4096, 2048], P(('group', 'chain')), may hold values from -6 to 6
- address_vectors: bfloat16 [4096, 2048], P(('group', 'chain')), may hold values from -6 to 6
- payload_vectors: bfloat16 [4096, 2048], P(('group', 'chain')), may hold values from -6 to 6
- unscaled_erase_address: bfloat16 [4096, 2048], P(('group', 'chain')), may hold values from -6 to 6
- adaptive_step_factor: bfloat16 [4096, 2048], P(('group', 'chain')), may hold values from 0 to 1
- fading_exponent: float32 [4096, 2048], P(('group', 'chain')), may hold values from -0.7 to 0
- diagonal_reward: float32 [32, 64], replicated, may hold values from -0.75 to 0.75
- standardize_scale: float32 [2048], replicated, may hold values from 0.5 to 1.5
- standardize_shift: float32 [2048], replicated, may hold values from -3 to 3
Outputs:
- output: bfloat16 [4096, 2048], P(('group', 'chain'))
The draws below stay inside these ranges and needn't reach their ends.
All inputs are finite; a program needn't handle non-finite values.
Results may differ from the reference program's by a relative error of at most 0.001.
Values sent between devices are 32-bit elements; how exact they have to be, the bound alone decides.
A program may use at most 320 MiB of HBM per device.

```python
import math
import jax
import jax.numpy as jnp
from jax import lax

DEVICE_SUBSPACES = 32
SUBSPACE_WIDTH = 64
T_DEV = 128
MODEL_WIDTH = 2048
TEXT_LENGTH = 4096


def head_pattern(key):
    slow_count = DEVICE_SUBSPACES // 2
    order = jax.random.permutation(jax.random.fold_in(key, 11), DEVICE_SUBSPACES)
    slow = order < slow_count
    spots = jax.random.randint(jax.random.fold_in(key, 13), (2,), 0, TEXT_LENGTH)
    return (slow, spots)


def draw_fading_exponent(key, part):
    slow, spots = head_pattern(key)
    fast_rate = jnp.exp(jax.random.uniform(jax.random.fold_in(key, 21), (DEVICE_SUBSPACES,), jnp.float32, math.log(1.0 / 50.0), math.log(1.0 / 20.0)))
    slow_rate = 0.5 / TEXT_LENGTH * jnp.exp(jax.random.uniform(jax.random.fold_in(key, 22), (DEVICE_SUBSPACES,), jnp.float32, math.log(0.5), math.log(2.0)))
    base = jnp.where(slow, slow_rate, fast_rate)
    device_factor = jnp.exp(jax.random.uniform(jax.random.fold_in(key, 23), (TEXT_LENGTH // T_DEV, 1, DEVICE_SUBSPACES, 1), jnp.float32, math.log(0.6), math.log(1.8)))
    rough = jax.random.uniform(jax.random.fold_in(key, 24), (TEXT_LENGTH // T_DEV, T_DEV, DEVICE_SUBSPACES, SUBSPACE_WIDTH), jnp.float32, 0.5, 1.5)
    rate = base[None, None, :, None] * device_factor * rough
    positions = jnp.arange(TEXT_LENGTH).reshape(TEXT_LENGTH // T_DEV, T_DEV, 1, 1)
    hits = jnp.logical_or(positions == spots[0], positions == spots[1]).astype(jnp.float32)
    return (-(rate + 0.5 * hits)).reshape(TEXT_LENGTH, DEVICE_SUBSPACES * SUBSPACE_WIDTH).astype(jnp.float32)


def draw_adaptive_step_factor(key, part):
    slow, spots = head_pattern(key)
    fast = jax.random.uniform(jax.random.fold_in(key, 31), (TEXT_LENGTH, DEVICE_SUBSPACES, SUBSPACE_WIDTH), jnp.float32, 0.05, 0.95)
    slow_scale = 16.0 / TEXT_LENGTH * jnp.exp(jax.random.uniform(jax.random.fold_in(key, 32), (TEXT_LENGTH, DEVICE_SUBSPACES, SUBSPACE_WIDTH), jnp.float32, math.log(0.5), math.log(2.0)))
    rates = jnp.where(slow[None, :, None], slow_scale, fast)
    return rates.reshape(TEXT_LENGTH, DEVICE_SUBSPACES * SUBSPACE_WIDTH).astype(jnp.bfloat16)


def level_of(own_key, shape, split, least, largest):
    def one(dim, parts):
        draws = jax.random.uniform(jax.random.fold_in(jax.random.fold_in(own_key, 6), dim), (parts,), jnp.float32, least / len(split), largest / len(split))
        return jnp.repeat(jnp.exp(draws), shape[dim] // parts).reshape((-1,) + (1,) * (len(shape) - dim - 1))

    loudness = one(*split[0])
    for cut in split[1:]:
        loudness = loudness * one(*cut)
    return loudness


def gaussian(key, extent, width, reach, shards=(), dtype=jnp.bfloat16):
    values = jax.random.normal(key, extent, jnp.float32) * width
    if len(shards) > 0:
        values = level_of(key, extent, shards, -0.22, 0.18) * values
    return jnp.clip(values, min=-reach, max=reach).astype(dtype)


def setup_inputs(seed: int = 0) -> dict:
    keys = jax.random.split(jax.random.key(seed), 10)
    return {
        "query_gates": gaussian(keys[0], (TEXT_LENGTH, MODEL_WIDTH), 1.0, 6.0, ((0, 32),)),
        "address_vectors": gaussian(keys[1], (TEXT_LENGTH, MODEL_WIDTH), 1.0, 6.0, ((0, 32),)),
        "payload_vectors": gaussian(keys[2], (TEXT_LENGTH, MODEL_WIDTH), 1.0, 6.0, ((0, 32),)),
        "unscaled_erase_address": gaussian(keys[3], (TEXT_LENGTH, MODEL_WIDTH), 1.0, 6.0, ((0, 32),)),
        "adaptive_step_factor": draw_adaptive_step_factor(jax.random.fold_in(keys[9], 71), 0),
        "fading_exponent": draw_fading_exponent(jax.random.fold_in(keys[9], 71), 0),
        "diagonal_reward": gaussian(keys[6], (DEVICE_SUBSPACES, SUBSPACE_WIDTH), SUBSPACE_WIDTH ** -0.5, 0.75, (), jnp.float32),
        "standardize_scale": jnp.clip(jax.random.uniform(keys[7], (MODEL_WIDTH,), jnp.float32, 0.5, 1.5), 0.5, 1.5),
        "standardize_shift": gaussian(keys[8], (MODEL_WIDTH,), 0.5, 3.0, (), jnp.float32),
    }


def headwise(array):
    return array.astype(jnp.float32).reshape(array.shape[0], DEVICE_SUBSPACES, SUBSPACE_WIDTH)

def advance(state, inputs):
    query_gate_vectors, address_weighted, payload_weighted, decay, kappa, strength = inputs
    removed = jnp.einsum('hvk,hk->hv', state, kappa, precision=lax.Precision.HIGHEST)
    state = state * decay[:, None, :] - removed[:, :, None] * strength[:, None, :] + payload_weighted[:, :, None] * address_weighted[:, None, :]
    mixed = jnp.einsum('hvk,hk->hv', state, query_gate_vectors, precision=lax.Precision.HIGHEST)
    return (state, mixed)

def reference(query_gates, address_vectors, payload_vectors, unscaled_erase_address, adaptive_step_factor, fading_exponent, diagonal_reward, standardize_scale, standardize_shift):
    query_gate_vectors = headwise(query_gates)
    address_weighted = headwise(address_vectors)
    payload_weighted = headwise(payload_vectors)
    raw_key = headwise(unscaled_erase_address)
    kappa = raw_key * lax.rsqrt(lax.optimization_barrier(jnp.sum(raw_key * raw_key, axis=-1, keepdims=True)) + 1e-06)
    strength = headwise(adaptive_step_factor) * kappa
    decay = jnp.exp(headwise(fading_exponent))
    start = jnp.zeros((DEVICE_SUBSPACES, SUBSPACE_WIDTH, SUBSPACE_WIDTH), jnp.float32)
    final_state, mixed = lax.scan(advance, start, (query_gate_vectors, address_weighted, payload_weighted, decay, kappa, strength))
    center = mixed - lax.optimization_barrier(jnp.mean(mixed, axis=-1, keepdims=True))
    variance = lax.optimization_barrier(jnp.mean(center * center, axis=-1, keepdims=True))
    standardized_result = center * lax.rsqrt(variance + 0.00064)
    diagonal_extra_term = lax.optimization_barrier(jnp.sum(query_gate_vectors * address_weighted * diagonal_reward[None], axis=-1, keepdims=True)) * payload_weighted
    mixer_result = standardized_result.reshape(TEXT_LENGTH, MODEL_WIDTH) * standardize_scale + standardize_shift + diagonal_extra_term.reshape(TEXT_LENGTH, MODEL_WIDTH)
    return mixer_result.astype(jnp.bfloat16)
```

```python
import functools

import jax
import jax.numpy as jnp
from jax import lax
from jax.experimental import pallas as pl
from jax.experimental.pallas import tpu as pltpu
from jax.sharding import PartitionSpec as P

HEADS = 32
WIDTH = 64
PAIRS = 2
f32 = jnp.float32
bf16 = jnp.bfloat16
NN = ((1,), (0,))
NT = ((1,), (1,))
TN = ((0,), (0,))
MESH = pl.DeviceIdType.MESH


def split(x):
    hi = x.astype(bf16)
    return hi, (x - hi.astype(f32)).astype(bf16)


def dot(a, b, dims=NN):
    return lax.dot_general(a, b, (dims, ((), ())), preferred_element_type=f32)


def cat(parts, axis):
    return jnp.concatenate(parts, axis=axis)


def dot3(a, b):
    ah, al = split(a)
    bh, bl = split(b)
    n = b.shape[1]
    right = cat([cat([bh, bl], 1), cat([bh, jnp.zeros_like(bl)], 1)], 0)
    r = dot(cat([ah, al], 1), right)
    return r[:, :n] + r[:, n:]


def column(row):
    return jnp.broadcast_to(row, (8, row.shape[1])).T[:, 0:1]


def local_kernel(q_ref, k_ref, v_ref, e_ref, a_ref, f_ref, u_ref, map_ref, local_ref, along_ref, extra_ref):
    T = q_ref.shape[0]
    row = lax.broadcasted_iota(jnp.int32, (T, T), 0)
    col = lax.broadcasted_iota(jnp.int32, (T, T), 1)
    strict = row < col
    through = row <= col
    top_mask = cat([strict.astype(f32), through.astype(f32)], 1) > 0.5
    differ = row ^ col
    tri = through.astype(bf16)
    tri2 = cat([tri, tri], 0)
    eye = (row == col).astype(f32)
    heads = range(2 * PAIRS)

    kb, rt, ks, ss, vs, kb_abs, rt_abs, kt, st, last = ([] for _ in range(10))
    for p in range(PAIRS):
        lanes = slice(2 * WIDTH * p, 2 * WIDTH * (p + 1))
        q, k, v, e, a = (ref[:, lanes].astype(f32).T for ref in (q_ref, k_ref, v_ref, e_ref, a_ref))
        f = f_ref[:, lanes].T
        u = column(u_ref[:, lanes])
        fh = f.astype(bf16)
        rest = f - fh.astype(f32)
        fm = rest.astype(bf16)
        fl = (rest - fm.astype(f32)).astype(bf16)
        c = dot(cat([fh, fm], 1), tri2) + dot(fl, tri)
        end = c[:, T - 1 : T]
        mid = 0.5 * end
        e_in = jnp.exp(c - mid)
        e_before = jnp.exp(c - f - mid)
        e_inv = jnp.exp(mid - c)
        g = jnp.exp(mid)
        final = jnp.exp(end)
        qku = q * k * u
        for i in range(2):
            r = slice(WIDTH * i, WIDTH * (i + 1))
            kap = e[r] * lax.rsqrt(jnp.sum(e[r] * e[r], axis=0, keepdims=True) + 1e-06)
            stren = a[r] * kap
            kb.append(kap * e_before[r])
            rt.append(q[r] * e_in[r])
            ks.append(k[r] * e_inv[r])
            ss.append(stren * e_inv[r])
            kb_abs.append(kb[-1] * g[r])
            rt_abs.append(rt[-1] * g[r])
            kt.append(ks[-1] * g[r])
            st.append(ss[-1] * g[r])
            last.append(final[r])
            vs.append(v[r].astype(bf16))
            extra_ref[2 * p + i] = jnp.sum(qku[r], axis=0, keepdims=True) * v[r]

    mixes = []
    for h in heads:
        lh, ll = split(cat([ks[h], ss[h]], 1))
        rh, rl = split(cat([kb[h], rt[h]], 1))
        mix = cat([lh, ll], 0).T
        mixes.append(dot(cat([mix, mix], 1), cat([rh, rh, rl, rl], 0)))
    lower = [jnp.where(strict, m[T:, :T], 0.0) for m in mixes]
    read_strength = [jnp.where(through, m[T:, T:], 0.0) for m in mixes]
    values = []
    for h in heads:
        th, tl = split(jnp.where(top_mask, mixes[h][:T], 0.0))
        values.append(dot(cat([vs[h], vs[h]], 1), cat([th, tl], 0)))
    inverse = [eye - jnp.where(differ == 1, low, 0.0) for low in lower]
    bit = 1
    while (2 << bit) <= T:
        here = (differ >> bit) == 1
        step = [dot3(inverse[h], jnp.where(here, lower[h], 0.0)) for h in heads]
        inverse = [inverse[h] - dot3(step[h], inverse[h]) for h in heads]
        bit += 1
    removed = [dot3(cat([values[h][:, :T], kb_abs[h]], 0), inverse[h]) for h in heads]
    read = [dot3(removed[h], read_strength[h]) for h in heads]
    krow = lax.broadcasted_iota(jnp.int32, (WIDTH, 2 * WIDTH), 0)
    kcol = lax.broadcasted_iota(jnp.int32, (WIDTH, 2 * WIDTH), 1)
    diagonal = kcol == krow + WIDTH
    for h in heads:
        local_ref[h] = values[h][:, T:] - read[h][:WIDTH]
        along_ref[h] = rt_abs[h] - read[h][WIDTH:]
        sh, sl = split(st[h])
        kh, kl = split(kt[h])
        wh, wl = split(removed[h])
        vpad = cat([vs[h], jnp.zeros_like(vs[h])], 0)
        gain = dot(cat([kh, kl], 1), cat([vpad, vpad], 1), NT)
        loss = dot(cat([sh, sl], 1), cat([wh, wh], 1), NT) + dot(sh, wl, NT)
        map_ref[h] = gain - loss + jnp.where(diagonal, last[h], 0.0)


def scan_kernel(axes, map_ref, state_ref, inbox, outbox, send1, recv1, send2, recv2):
    (outer_axis, outer), (inner_axis, inner) = axes
    total = outer * inner
    owners = min(total, HEADS)
    share = HEADS // owners
    stride = total // owners
    me = lax.axis_index(outer_axis) * inner + lax.axis_index(inner_axis)
    mine = me // stride
    half = WIDTH // 2

    def place(d):
        return (d // inner, lax.rem(d, inner))

    def when(condition, body):
        if condition is True:
            body()
        else:
            pl.when(condition)(body)

    own = True if stride == 1 else lax.rem(me, stride) == 0

    barrier = pltpu.get_barrier_semaphore()

    def greet_owner(j, _):
        when(j * stride != me, lambda: pl.semaphore_signal(barrier, inc=1, device_id=place(j * stride), device_id_type=MESH))
        return 0

    def greet_rest(d, _):
        when(lax.rem(d, stride) != 0, lambda: pl.semaphore_signal(barrier, inc=1, device_id=place(d), device_id_type=MESH))
        return 0

    lax.fori_loop(0, owners, greet_owner, 0)
    if stride == 1:
        pl.semaphore_wait(barrier, total - 1)
    else:

        def greet():
            lax.fori_loop(0, total, greet_rest, 0)
            pl.semaphore_wait(barrier, total - 1)

        when(own, greet)
        when(lax.rem(me, stride) != 0, lambda: pl.semaphore_wait(barrier, owners))

    def to_owner(j):
        return pltpu.make_async_remote_copy(
            src_ref=map_ref.at[pl.ds(j * share, share)],
            dst_ref=inbox.at[me],
            send_sem=send1.at[j],
            recv_sem=recv1.at[me],
            device_id=place(j * stride),
            device_id_type=MESH,
        )

    def from_device(d):
        return pltpu.make_async_remote_copy(
            src_ref=map_ref.at[pl.ds(0, share)],
            dst_ref=inbox.at[d],
            send_sem=send1.at[0],
            recv_sem=recv1.at[d],
            device_id=place(d),
            device_id_type=MESH,
        )

    def to_device(d):
        return pltpu.make_async_remote_copy(
            src_ref=outbox.at[d],
            dst_ref=state_ref.at[pl.ds(mine * share, share)],
            send_sem=send2.at[d],
            recv_sem=recv2.at[mine],
            device_id=place(d),
            device_id_type=MESH,
        )

    def from_owner(j):
        return pltpu.make_async_remote_copy(
            src_ref=outbox.at[0],
            dst_ref=state_ref.at[pl.ds(j * share, share)],
            send_sem=send2.at[0],
            recv_sem=recv2.at[j],
            device_id=place(j * stride),
            device_id_type=MESH,
        )

    def send_map(n, _):
        j = lax.rem(mine + n, owners)
        when(j * stride != me, lambda: to_owner(j).start())
        return 0

    lax.fori_loop(0, owners, send_map, 0)

    def scan():
        for i in range(share):
            inbox[me, i] = map_ref[mine * share + i]

        def advance(d, states):
            when(d != me, lambda: from_device(d).wait_recv())
            new = []
            for i, s in enumerate(states):
                outbox[d, i] = cat([s[:half], s[half:]], 1)
                m = inbox[d, i]
                mh, ml = split(m)
                sh, sl = split(s)
                zero = jnp.zeros_like(sh)
                moved = dot(cat([mh, ml], 1), cat([zero, sh, zero, sh], 0)) + dot(mh, cat([zero, sl], 0))
                new.append(m[:, :WIDTH] + moved)
            return tuple(new)

        lax.fori_loop(0, total, advance, tuple(jnp.zeros((WIDTH, WIDTH), f32) for _ in range(share)))
        for i in range(share):
            state_ref[mine * share + i] = outbox[me, i]

        def send_state(n, _):
            to_device(lax.rem(me + n, total)).start()
            return 0

        lax.fori_loop(1, total, send_state, 0)

    when(own, scan)

    def finish_owner(j, _):
        def body():
            from_owner(j).wait_recv()
            to_owner(j).wait_send()

        when(j * stride != me, body)
        return 0

    lax.fori_loop(0, owners, finish_owner, 0)

    def finish_states():
        def finish_device(n, _):
            to_device(lax.rem(me + n, total)).wait_send()
            return 0

        lax.fori_loop(1, total, finish_device, 0)

    when(own, finish_states)


def final_kernel(state_ref, local_ref, along_ref, extra_ref, scale_ref, shift_ref, out_ref):
    half = WIDTH // 2
    for p in range(PAIRS):
        lanes = slice(2 * WIDTH * p, 2 * WIDTH * (p + 1))
        parts = []
        for h in (2 * p, 2 * p + 1):
            packed = state_ref[h]
            s = cat([packed[:, :WIDTH], packed[:, WIDTH:]], 0)
            sh, sl = split(s)
            ah, al = split(along_ref[h])
            mixed = local_ref[h] + dot(cat([sh, sh, sl], 0), cat([ah, al, ah], 0), TN)
            center = mixed - jnp.mean(mixed, axis=0, keepdims=True)
            variance = jnp.mean(center * center, axis=0, keepdims=True)
            parts.append(center * lax.rsqrt(variance + 0.00064))
        normed = cat(parts, 0) * column(scale_ref[:, lanes]) + column(shift_ref[:, lanes])
        normed = normed + cat([extra_ref[2 * p], extra_ref[2 * p + 1]], 0)
        out_ref[:, lanes] = normed.T.astype(out_ref.dtype)


def per_device(axes, q, k, v, e, a, f, reward, scale, shift):
    rows, columns = q.shape
    total = axes[0][1] * axes[1][1]
    owners = min(total, HEADS)
    share = HEADS // owners
    lanes = 2 * WIDTH * PAIRS
    steps = columns // lanes
    tokens = pl.BlockSpec((rows, lanes), lambda i: (0, i))
    vector = pl.BlockSpec((1, lanes), lambda i: (0, i))
    def per_head(n, m):
        return pl.BlockSpec((2 * PAIRS, n, m), lambda i: (i, 0, 0))

    maps, local, along, extra = pl.pallas_call(
        local_kernel,
        grid=(steps,),
        in_specs=[tokens] * 6 + [vector],
        out_specs=[per_head(WIDTH, 2 * WIDTH)] + [per_head(WIDTH, rows)] * 3,
        out_shape=[jax.ShapeDtypeStruct((HEADS, WIDTH, 2 * WIDTH), f32)]
        + [jax.ShapeDtypeStruct((HEADS, WIDTH, rows), f32)] * 3,
        compiler_params=pltpu.CompilerParams(vmem_limit_bytes=48 * 2**20),
        name="local",
    )(q, k, v, e, a, f, reward.reshape(1, columns))

    states = pl.pallas_call(
        functools.partial(scan_kernel, axes),
        in_specs=[pl.BlockSpec(memory_space=pltpu.VMEM)],
        out_specs=pl.BlockSpec(memory_space=pltpu.VMEM),
        out_shape=jax.ShapeDtypeStruct((HEADS, WIDTH // 2, 2 * WIDTH), f32),
        scratch_shapes=[
            pltpu.VMEM((total, share, WIDTH, 2 * WIDTH), f32),
            pltpu.VMEM((total, share, WIDTH // 2, 2 * WIDTH), f32),
            pltpu.SemaphoreType.DMA((owners,)),
            pltpu.SemaphoreType.DMA((total,)),
            pltpu.SemaphoreType.DMA((total,)),
            pltpu.SemaphoreType.DMA((owners,)),
        ],
        compiler_params=pltpu.CompilerParams(
            collective_id=0, has_side_effects=True, vmem_limit_bytes=48 * 2**20
        ),
        name="scan",
    )(maps)

    return pl.pallas_call(
        final_kernel,
        grid=(steps,),
        in_specs=[per_head(WIDTH // 2, 2 * WIDTH)] + [per_head(WIDTH, rows)] * 3 + [vector] * 2,
        out_specs=tokens,
        out_shape=jax.ShapeDtypeStruct((rows, columns), bf16),
        compiler_params=pltpu.CompilerParams(vmem_limit_bytes=48 * 2**20),
        name="final",
    )(states, local, along, extra, scale.reshape(1, columns), shift.reshape(1, columns))


def solution(mesh):
    axes = tuple((name, mesh.shape[name]) for name in mesh.axis_names)
    placed = (P(axes_names(mesh), None),) * 6 + (P(),) * 3
    return jax.shard_map(
        functools.partial(per_device, axes),
        mesh=mesh,
        in_specs=placed,
        out_specs=P(axes_names(mesh), None),
        check_vma=False,
    )


def axes_names(mesh):
    return tuple(mesh.axis_names)
```

```python
import functools

import jax
import jax.numpy as jnp
from jax import lax
from jax.experimental import pallas as pl
from jax.experimental.pallas import tpu as pltpu
from jax.sharding import PartitionSpec as P

HEADS = 32
WIDTH = 64
PAIRS = 2
f32 = jnp.float32
bf16 = jnp.bfloat16
NN = ((1,), (0,))
NT = ((1,), (1,))
TN = ((0,), (0,))
MESH = pl.DeviceIdType.MESH


def split(x):
    hi = x.astype(bf16)
    return hi, (x - hi.astype(f32)).astype(bf16)


def dot(a, b, dims=NN):
    return lax.dot_general(a, b, (dims, ((), ())), preferred_element_type=f32)


def cat(parts, axis):
    return jnp.concatenate(parts, axis=axis)


def dot3(a, b):
    ah, al = split(a)
    bh, bl = split(b)
    n = b.shape[1]
    right = cat([cat([bh, bl], 1), cat([bh, jnp.zeros_like(bl)], 1)], 0)
    r = dot(cat([ah, al], 1), right)
    return r[:, :n] + r[:, n:]


def column(row):
    return jnp.broadcast_to(row, (8, row.shape[1])).T[:, 0:1]


def local_kernel(q_ref, k_ref, v_ref, e_ref, a_ref, f_ref, u_ref, map_ref, local_ref, along_ref, extra_ref):
    T = q_ref.shape[0]
    row = lax.broadcasted_iota(jnp.int32, (T, T), 0)
    col = lax.broadcasted_iota(jnp.int32, (T, T), 1)
    strict = row < col
    through = row <= col
    top_mask = cat([strict.astype(f32), through.astype(f32)], 1) > 0.5
    differ = row ^ col
    tri = through.astype(bf16)
    tri2 = cat([tri, tri], 0)
    eye = (row == col).astype(f32)
    heads = range(2 * PAIRS)

    kb, rt, ks, ss, vs, kb_abs, rt_abs, kt, st, last = ([] for _ in range(10))
    for p in range(PAIRS):
        lanes = slice(2 * WIDTH * p, 2 * WIDTH * (p + 1))
        q, k, v, e, a = (ref[:, lanes].astype(f32).T for ref in (q_ref, k_ref, v_ref, e_ref, a_ref))
        f = f_ref[:, lanes].T
        u = column(u_ref[:, lanes])
        fh = f.astype(bf16)
        rest = f - fh.astype(f32)
        fm = rest.astype(bf16)
        fl = (rest - fm.astype(f32)).astype(bf16)
        c = dot(cat([fh, fm], 1), tri2) + dot(fl, tri)
        end = c[:, T - 1 : T]
        mid = 0.5 * end
        e_in = jnp.exp(c - mid)
        e_before = jnp.exp(c - f - mid)
        e_inv = jnp.exp(mid - c)
        g = jnp.exp(mid)
        final = jnp.exp(end)
        qku = q * k * u
        for i in range(2):
            r = slice(WIDTH * i, WIDTH * (i + 1))
            kap = e[r] * lax.rsqrt(jnp.sum(e[r] * e[r], axis=0, keepdims=True) + 1e-06)
            stren = a[r] * kap
            kb.append(kap * e_before[r])
            rt.append(q[r] * e_in[r])
            ks.append(k[r] * e_inv[r])
            ss.append(stren * e_inv[r])
            kb_abs.append(kb[-1] * g[r])
            rt_abs.append(rt[-1] * g[r])
            kt.append(ks[-1] * g[r])
            st.append(ss[-1] * g[r])
            last.append(final[r])
            vs.append(v[r].astype(bf16))
            extra_ref[2 * p + i] = jnp.sum(qku[r], axis=0, keepdims=True) * v[r]

    mixes = []
    for h in heads:
        lh, ll = split(cat([ks[h], ss[h]], 1))
        rh, rl = split(cat([kb[h], rt[h]], 1))
        mix = cat([lh, ll], 0).T
        mixes.append(dot(cat([mix, mix], 1), cat([rh, rh, rl, rl], 0)))
    lower = [jnp.where(strict, m[T:, :T], 0.0) for m in mixes]
    read_strength = [jnp.where(through, m[T:, T:], 0.0) for m in mixes]
    values = []
    for h in heads:
        th, tl = split(jnp.where(top_mask, mixes[h][:T], 0.0))
        values.append(dot(cat([vs[h], vs[h]], 1), cat([th, tl], 0)))
    inverse = [eye - jnp.where(differ == 1, low, 0.0) for low in lower]
    bit = 1
    while (2 << bit) <= T:
        here = (differ >> bit) == 1
        step = [dot3(inverse[h], jnp.where(here, lower[h], 0.0)) for h in heads]
        inverse = [inverse[h] - dot3(step[h], inverse[h]) for h in heads]
        bit += 1
    removed = [dot3(cat([values[h][:, :T], kb_abs[h]], 0), inverse[h]) for h in heads]
    read = [dot3(removed[h], read_strength[h]) for h in heads]
    krow = lax.broadcasted_iota(jnp.int32, (WIDTH, 2 * WIDTH), 0)
    kcol = lax.broadcasted_iota(jnp.int32, (WIDTH, 2 * WIDTH), 1)
    diagonal = kcol == krow + WIDTH
    for h in heads:
        local_ref[h] = values[h][:, T:] - read[h][:WIDTH]
        along_ref[h] = rt_abs[h] - read[h][WIDTH:]
        sh, sl = split(st[h])
        kh, kl = split(kt[h])
        wh, wl = split(removed[h])
        vpad = cat([vs[h], jnp.zeros_like(vs[h])], 0)
        gain = dot(cat([kh, kl], 1), cat([vpad, vpad], 1), NT)
        loss = dot(cat([sh, sl], 1), cat([wh, wh], 1), NT) + dot(sh, wl, NT)
        map_ref[h] = gain - loss + jnp.where(diagonal, last[h], 0.0)


def scan_kernel(axes, map_ref, state_ref, inbox, outbox, prefix, send1, recv1, send2, recv2):
    (outer_axis, outer), (inner_axis, inner) = axes
    total = outer * inner
    owners = min(total, HEADS)
    share = HEADS // owners
    stride = total // owners
    me = lax.axis_index(outer_axis) * inner + lax.axis_index(inner_axis)
    mine = me // stride
    half = WIDTH // 2

    def place(d):
        return (d // inner, lax.rem(d, inner))

    def when(condition, body):
        if condition is True:
            body()
        else:
            pl.when(condition)(body)

    own = True if stride == 1 else lax.rem(me, stride) == 0

    barrier = pltpu.get_barrier_semaphore()

    def greet_owner(j, _):
        when(j * stride != me, lambda: pl.semaphore_signal(barrier, inc=1, device_id=place(j * stride), device_id_type=MESH))
        return 0

    def greet_rest(d, _):
        when(lax.rem(d, stride) != 0, lambda: pl.semaphore_signal(barrier, inc=1, device_id=place(d), device_id_type=MESH))
        return 0

    lax.fori_loop(0, owners, greet_owner, 0)
    if stride == 1:
        pl.semaphore_wait(barrier, total - 1)
    else:

        def greet():
            lax.fori_loop(0, total, greet_rest, 0)
            pl.semaphore_wait(barrier, total - 1)

        when(own, greet)
        when(lax.rem(me, stride) != 0, lambda: pl.semaphore_wait(barrier, owners))

    def to_owner(j):
        return pltpu.make_async_remote_copy(
            src_ref=map_ref.at[pl.ds(j * share, share)],
            dst_ref=inbox.at[me],
            send_sem=send1.at[j],
            recv_sem=recv1.at[me],
            device_id=place(j * stride),
            device_id_type=MESH,
        )

    def from_device(d):
        return pltpu.make_async_remote_copy(
            src_ref=map_ref.at[pl.ds(0, share)],
            dst_ref=inbox.at[d],
            send_sem=send1.at[0],
            recv_sem=recv1.at[d],
            device_id=place(d),
            device_id_type=MESH,
        )

    def to_device(d):
        return pltpu.make_async_remote_copy(
            src_ref=outbox.at[d],
            dst_ref=state_ref.at[pl.ds(mine * share, share)],
            send_sem=send2.at[d],
            recv_sem=recv2.at[mine],
            device_id=place(d),
            device_id_type=MESH,
        )

    def from_owner(j):
        return pltpu.make_async_remote_copy(
            src_ref=outbox.at[0],
            dst_ref=state_ref.at[pl.ds(j * share, share)],
            send_sem=send2.at[0],
            recv_sem=recv2.at[j],
            device_id=place(j * stride),
            device_id_type=MESH,
        )

    def send_map(n, _):
        j = lax.rem(mine + n, owners)
        when(j * stride != me, lambda: to_owner(j).start())
        return 0

    lax.fori_loop(0, owners, send_map, 0)

    def scan():
        for i in range(share):
            inbox[me, i] = map_ref[mine * share + i]

        def arrive(d, _):
            when(d != me, lambda: from_device(d).wait_recv())
            return 0

        lax.fori_loop(0, total, arrive, 0)
        segments = 4 if total % 4 == 0 else 1
        length = total // segments
        krow = lax.broadcasted_iota(jnp.int32, (WIDTH, 2 * WIDTH), 0)
        kcol = lax.broadcasted_iota(jnp.int32, (WIDTH, 2 * WIDTH), 1)
        unit = (kcol == krow + WIDTH).astype(f32)
        offset = kcol < WIDTH

        def right_side(s):
            sh, sl = split(s)
            zero = jnp.zeros_like(sh)
            return cat([zero, sh, zero, sh], 0), cat([zero, sl], 0)

        def apply(m, right):
            mh, ml = split(m)
            return dot(cat([mh, ml], 1), right[0]) + dot(mh, right[1])

        for i in range(share):

            def advance(t, before):
                after = []
                for g in range(segments):
                    d = g * length + t
                    prefix[d] = before[g]
                    m = inbox[d, i]
                    after.append(apply(m, right_side(before[g])) + jnp.where(offset, m, 0.0))
                return tuple(after)

            ends = lax.fori_loop(0, length, advance, (unit,) * segments)
            s = jnp.zeros((WIDTH, WIDTH), f32)
            rights = []
            for g in range(segments):
                rights.append(right_side(s))
                s = apply(ends[g], rights[g]) + ends[g][:, :WIDTH]

            def place_states(t, _):
                for g in range(segments):
                    d = g * length + t
                    m = prefix[d]
                    s = apply(m, rights[g]) + m[:, :WIDTH]
                    outbox[d, i] = cat([s[:half], s[half:]], 1)
                return 0

            lax.fori_loop(0, length, place_states, 0)

        for i in range(share):
            state_ref[mine * share + i] = outbox[me, i]

        def send_state(n, _):
            to_device(lax.rem(me + n, total)).start()
            return 0

        lax.fori_loop(1, total, send_state, 0)

    when(own, scan)

    def finish_owner(j, _):
        def body():
            from_owner(j).wait_recv()
            to_owner(j).wait_send()

        when(j * stride != me, body)
        return 0

    lax.fori_loop(0, owners, finish_owner, 0)

    def finish_states():
        def finish_device(n, _):
            to_device(lax.rem(me + n, total)).wait_send()
            return 0

        lax.fori_loop(1, total, finish_device, 0)

    when(own, finish_states)


def final_kernel(state_ref, local_ref, along_ref, extra_ref, scale_ref, shift_ref, out_ref):
    half = WIDTH // 2
    for p in range(PAIRS):
        lanes = slice(2 * WIDTH * p, 2 * WIDTH * (p + 1))
        parts = []
        for h in (2 * p, 2 * p + 1):
            packed = state_ref[h]
            s = cat([packed[:, :WIDTH], packed[:, WIDTH:]], 0)
            sh, sl = split(s)
            ah, al = split(along_ref[h])
            mixed = local_ref[h] + dot(cat([sh, sh, sl], 0), cat([ah, al, ah], 0), TN)
            center = mixed - jnp.mean(mixed, axis=0, keepdims=True)
            variance = jnp.mean(center * center, axis=0, keepdims=True)
            parts.append(center * lax.rsqrt(variance + 0.00064))
        normed = cat(parts, 0) * column(scale_ref[:, lanes]) + column(shift_ref[:, lanes])
        normed = normed + cat([extra_ref[2 * p], extra_ref[2 * p + 1]], 0)
        out_ref[:, lanes] = normed.T.astype(out_ref.dtype)


def per_device(axes, q, k, v, e, a, f, reward, scale, shift):
    rows, columns = q.shape
    total = axes[0][1] * axes[1][1]
    owners = min(total, HEADS)
    share = HEADS // owners
    lanes = 2 * WIDTH * PAIRS
    steps = columns // lanes
    tokens = pl.BlockSpec((rows, lanes), lambda i: (0, i))
    vector = pl.BlockSpec((1, lanes), lambda i: (0, i))
    def per_head(n, m):
        return pl.BlockSpec((2 * PAIRS, n, m), lambda i: (i, 0, 0))

    maps, local, along, extra = pl.pallas_call(
        local_kernel,
        grid=(steps,),
        in_specs=[tokens] * 6 + [vector],
        out_specs=[per_head(WIDTH, 2 * WIDTH)] + [per_head(WIDTH, rows)] * 3,
        out_shape=[jax.ShapeDtypeStruct((HEADS, WIDTH, 2 * WIDTH), f32)]
        + [jax.ShapeDtypeStruct((HEADS, WIDTH, rows), f32)] * 3,
        compiler_params=pltpu.CompilerParams(vmem_limit_bytes=62 * 2**20),
        name="local",
    )(q, k, v, e, a, f, reward.reshape(1, columns))

    states = pl.pallas_call(
        functools.partial(scan_kernel, axes),
        in_specs=[pl.BlockSpec(memory_space=pltpu.VMEM)],
        out_specs=pl.BlockSpec(memory_space=pltpu.VMEM),
        out_shape=jax.ShapeDtypeStruct((HEADS, WIDTH // 2, 2 * WIDTH), f32),
        scratch_shapes=[
            pltpu.VMEM((total, share, WIDTH, 2 * WIDTH), f32),
            pltpu.VMEM((total, share, WIDTH // 2, 2 * WIDTH), f32),
            pltpu.VMEM((total, WIDTH, 2 * WIDTH), f32),
            pltpu.SemaphoreType.DMA((owners,)),
            pltpu.SemaphoreType.DMA((total,)),
            pltpu.SemaphoreType.DMA((total,)),
            pltpu.SemaphoreType.DMA((owners,)),
        ],
        compiler_params=pltpu.CompilerParams(
            collective_id=0, has_side_effects=True, vmem_limit_bytes=48 * 2**20
        ),
        name="scan",
    )(maps)

    return pl.pallas_call(
        final_kernel,
        grid=(steps,),
        in_specs=[per_head(WIDTH // 2, 2 * WIDTH)] + [per_head(WIDTH, rows)] * 3 + [vector] * 2,
        out_specs=tokens,
        out_shape=jax.ShapeDtypeStruct((rows, columns), bf16),
        compiler_params=pltpu.CompilerParams(vmem_limit_bytes=62 * 2**20),
        name="final",
    )(states, local, along, extra, scale.reshape(1, columns), shift.reshape(1, columns))


def solution(mesh):
    axes = tuple((name, mesh.shape[name]) for name in mesh.axis_names)
    placed = (P(axes_names(mesh), None),) * 6 + (P(),) * 3
    return jax.shard_map(
        functools.partial(per_device, axes),
        mesh=mesh,
        in_specs=placed,
        out_specs=P(axes_names(mesh), None),
        check_vma=False,
    )


def axes_names(mesh):
    return tuple(mesh.axis_names)
```

```python
import functools

import jax
import jax.numpy as jnp
from jax import lax
from jax.experimental import pallas as pl
from jax.experimental.pallas import tpu as pltpu
from jax.sharding import PartitionSpec as P

HEADS = 32
WIDTH = 64
PAIRS = 4
f32 = jnp.float32
bf16 = jnp.bfloat16
NN = ((1,), (0,))
NT = ((1,), (1,))
TN = ((0,), (0,))
MESH = pl.DeviceIdType.MESH


def split(x):
    hi = x.astype(bf16)
    return hi, (x - hi.astype(f32)).astype(bf16)


def dot(a, b, dims=NN):
    return lax.dot_general(a, b, (dims, ((), ())), preferred_element_type=f32)


def cat(parts, axis):
    return jnp.concatenate(parts, axis=axis)


def dot3(a, b):
    ah, al = split(a)
    bh, bl = split(b)
    n = b.shape[1]
    right = cat([cat([bh, bl], 1), cat([bh, jnp.zeros_like(bl)], 1)], 0)
    r = dot(cat([ah, al], 1), right)
    return r[:, :n] + r[:, n:]


def column(row):
    return jnp.broadcast_to(row, (8, row.shape[1])).T[:, 0:1]


def local_kernel(q_ref, k_ref, v_ref, e_ref, a_ref, f_ref, u_ref, map_ref, local_ref, along_ref, extra_ref):
    T = q_ref.shape[0]
    row = lax.broadcasted_iota(jnp.int32, (T, T), 0)
    col = lax.broadcasted_iota(jnp.int32, (T, T), 1)
    strict = row < col
    through = row <= col
    top_mask = cat([strict.astype(f32), through.astype(f32)], 1) > 0.5
    differ = row ^ col
    tri = through.astype(bf16)
    tri2 = cat([tri, tri], 0)
    eye = (row == col).astype(f32)
    heads = range(2 * PAIRS)

    kb, rt, ks, ss, vs, kb_abs, rt_abs, kt, st, last = ([] for _ in range(10))
    for p in range(PAIRS):
        lanes = slice(2 * WIDTH * p, 2 * WIDTH * (p + 1))
        q, k, v, e, a = (ref[:, lanes].astype(f32).T for ref in (q_ref, k_ref, v_ref, e_ref, a_ref))
        f = f_ref[:, lanes].T
        u = column(u_ref[:, lanes])
        fh = f.astype(bf16)
        rest = f - fh.astype(f32)
        fm = rest.astype(bf16)
        fl = (rest - fm.astype(f32)).astype(bf16)
        c = dot(cat([fh, fm], 1), tri2) + dot(fl, tri)
        end = c[:, T - 1 : T]
        mid = 0.5 * end
        e_in = jnp.exp(c - mid)
        e_before = jnp.exp(c - f - mid)
        e_inv = jnp.exp(mid - c)
        g = jnp.exp(mid)
        final = jnp.exp(end)
        qku = q * k * u
        for i in range(2):
            r = slice(WIDTH * i, WIDTH * (i + 1))
            kap = e[r] * lax.rsqrt(jnp.sum(e[r] * e[r], axis=0, keepdims=True) + 1e-06)
            stren = a[r] * kap
            kb.append(kap * e_before[r])
            rt.append(q[r] * e_in[r])
            ks.append(k[r] * e_inv[r])
            ss.append(stren * e_inv[r])
            kb_abs.append(kb[-1] * g[r])
            rt_abs.append(rt[-1] * g[r])
            kt.append(ks[-1] * g[r])
            st.append(ss[-1] * g[r])
            last.append(final[r])
            vs.append(v[r].astype(bf16))
            extra_ref[2 * p + i] = jnp.sum(qku[r], axis=0, keepdims=True) * v[r]

    mixes = []
    for h in heads:
        lh, ll = split(cat([ks[h], ss[h]], 1))
        rh, rl = split(cat([kb[h], rt[h]], 1))
        mix = cat([lh, ll], 0).T
        mixes.append(dot(cat([mix, mix], 1), cat([rh, rh, rl, rl], 0)))
    lower = [jnp.where(strict, m[T:, :T], 0.0) for m in mixes]
    read_strength = [jnp.where(through, m[T:, T:], 0.0) for m in mixes]
    values = []
    for h in heads:
        th, tl = split(jnp.where(top_mask, mixes[h][:T], 0.0))
        values.append(dot(cat([vs[h], vs[h]], 1), cat([th, tl], 0)))
    inverse = [eye - jnp.where(differ == 1, low, 0.0) for low in lower]
    bit = 1
    while (2 << bit) <= T:
        here = (differ >> bit) == 1
        step = [dot3(inverse[h], jnp.where(here, lower[h], 0.0)) for h in heads]
        inverse = [inverse[h] - dot3(step[h], inverse[h]) for h in heads]
        bit += 1
    removed = [dot3(cat([values[h][:, :T], kb_abs[h]], 0), inverse[h]) for h in heads]
    read = [dot3(removed[h], read_strength[h]) for h in heads]
    krow = lax.broadcasted_iota(jnp.int32, (WIDTH, 2 * WIDTH), 0)
    kcol = lax.broadcasted_iota(jnp.int32, (WIDTH, 2 * WIDTH), 1)
    diagonal = kcol == krow + WIDTH
    for h in heads:
        local_ref[h] = values[h][:, T:] - read[h][:WIDTH]
        along_ref[h] = rt_abs[h] - read[h][WIDTH:]
        sh, sl = split(st[h])
        kh, kl = split(kt[h])
        wh, wl = split(removed[h])
        vpad = cat([vs[h], jnp.zeros_like(vs[h])], 0)
        gain = dot(cat([kh, kl], 1), cat([vpad, vpad], 1), NT)
        loss = dot(cat([sh, sl], 1), cat([wh, wh], 1), NT) + dot(sh, wl, NT)
        map_ref[h] = gain - loss + jnp.where(diagonal, last[h], 0.0)


def scan_kernel(axes, map_ref, state_ref, inbox, outbox, prefix, send1, recv1, send2, recv2):
    (outer_axis, outer), (inner_axis, inner) = axes
    total = outer * inner
    owners = min(total, HEADS)
    share = HEADS // owners
    stride = total // owners
    me = lax.axis_index(outer_axis) * inner + lax.axis_index(inner_axis)
    mine = me // stride
    half = WIDTH // 2

    def place(d):
        return (d // inner, lax.rem(d, inner))

    def when(condition, body):
        if condition is True:
            body()
        else:
            pl.when(condition)(body)

    own = True if stride == 1 else lax.rem(me, stride) == 0

    barrier = pltpu.get_barrier_semaphore()

    def greet_owner(j, _):
        when(j * stride != me, lambda: pl.semaphore_signal(barrier, inc=1, device_id=place(j * stride), device_id_type=MESH))
        return 0

    def greet_rest(d, _):
        when(lax.rem(d, stride) != 0, lambda: pl.semaphore_signal(barrier, inc=1, device_id=place(d), device_id_type=MESH))
        return 0

    lax.fori_loop(0, owners, greet_owner, 0)
    if stride == 1:
        pl.semaphore_wait(barrier, total - 1)
    else:

        def greet():
            lax.fori_loop(0, total, greet_rest, 0)
            pl.semaphore_wait(barrier, total - 1)

        when(own, greet)
        when(lax.rem(me, stride) != 0, lambda: pl.semaphore_wait(barrier, owners))

    def to_owner(j):
        return pltpu.make_async_remote_copy(
            src_ref=map_ref.at[pl.ds(j * share, share)],
            dst_ref=inbox.at[me],
            send_sem=send1.at[j],
            recv_sem=recv1.at[me],
            device_id=place(j * stride),
            device_id_type=MESH,
        )

    def from_device(d):
        return pltpu.make_async_remote_copy(
            src_ref=map_ref.at[pl.ds(0, share)],
            dst_ref=inbox.at[d],
            send_sem=send1.at[0],
            recv_sem=recv1.at[d],
            device_id=place(d),
            device_id_type=MESH,
        )

    def to_device(d):
        return pltpu.make_async_remote_copy(
            src_ref=outbox.at[d],
            dst_ref=state_ref.at[pl.ds(mine * share, share)],
            send_sem=send2.at[d],
            recv_sem=recv2.at[mine],
            device_id=place(d),
            device_id_type=MESH,
        )

    def from_owner(j):
        return pltpu.make_async_remote_copy(
            src_ref=outbox.at[0],
            dst_ref=state_ref.at[pl.ds(j * share, share)],
            send_sem=send2.at[0],
            recv_sem=recv2.at[j],
            device_id=place(j * stride),
            device_id_type=MESH,
        )

    def send_map(n, _):
        j = lax.rem(mine + n, owners)
        when(j * stride != me, lambda: to_owner(j).start())
        return 0

    lax.fori_loop(0, owners, send_map, 0)

    def scan():
        for i in range(share):
            inbox[me, i] = map_ref[mine * share + i]

        def arrive(d, _):
            when(d != me, lambda: from_device(d).wait_recv())
            return 0

        lax.fori_loop(0, total, arrive, 0)
        segments = 4 if total % 4 == 0 else 1
        length = total // segments
        krow = lax.broadcasted_iota(jnp.int32, (WIDTH, 2 * WIDTH), 0)
        kcol = lax.broadcasted_iota(jnp.int32, (WIDTH, 2 * WIDTH), 1)
        unit = (kcol == krow + WIDTH).astype(f32)
        offset = kcol < WIDTH

        def right_side(s):
            sh, sl = split(s)
            zero = jnp.zeros_like(sh)
            return cat([zero, sh, zero, sh], 0), cat([zero, sl], 0)

        def apply(m, right):
            mh, ml = split(m)
            return dot(cat([mh, ml], 1), right[0]) + dot(mh, right[1])

        for i in range(share):

            def advance(t, before):
                after = []
                for g in range(segments):
                    d = g * length + t
                    prefix[d] = before[g]
                    m = inbox[d, i]
                    after.append(apply(m, right_side(before[g])) + jnp.where(offset, m, 0.0))
                return tuple(after)

            ends = lax.fori_loop(0, length, advance, (unit,) * segments)
            s = jnp.zeros((WIDTH, WIDTH), f32)
            rights = []
            for g in range(segments):
                rights.append(right_side(s))
                s = apply(ends[g], rights[g]) + ends[g][:, :WIDTH]

            def place_states(t, _):
                for g in range(segments):
                    d = g * length + t
                    m = prefix[d]
                    s = apply(m, rights[g]) + m[:, :WIDTH]
                    outbox[d, i] = cat([s[:half], s[half:]], 1)
                return 0

            lax.fori_loop(0, length, place_states, 0)

        for i in range(share):
            state_ref[mine * share + i] = outbox[me, i]

        def send_state(n, _):
            to_device(lax.rem(me + n, total)).start()
            return 0

        lax.fori_loop(1, total, send_state, 0)

    when(own, scan)

    def finish_owner(j, _):
        def body():
            from_owner(j).wait_recv()
            to_owner(j).wait_send()

        when(j * stride != me, body)
        return 0

    lax.fori_loop(0, owners, finish_owner, 0)

    def finish_states():
        def finish_device(n, _):
            to_device(lax.rem(me + n, total)).wait_send()
            return 0

        lax.fori_loop(1, total, finish_device, 0)

    when(own, finish_states)


def final_kernel(state_ref, local_ref, along_ref, extra_ref, scale_ref, shift_ref, out_ref):
    half = WIDTH // 2
    for p in range(PAIRS):
        lanes = slice(2 * WIDTH * p, 2 * WIDTH * (p + 1))
        parts = []
        for h in (2 * p, 2 * p + 1):
            packed = state_ref[h]
            s = cat([packed[:, :WIDTH], packed[:, WIDTH:]], 0)
            sh, sl = split(s)
            ah, al = split(along_ref[h])
            mixed = local_ref[h] + dot(cat([sh, sh, sl], 0), cat([ah, al, ah], 0), TN)
            center = mixed - jnp.mean(mixed, axis=0, keepdims=True)
            variance = jnp.mean(center * center, axis=0, keepdims=True)
            parts.append(center * lax.rsqrt(variance + 0.00064))
        normed = cat(parts, 0) * column(scale_ref[:, lanes]) + column(shift_ref[:, lanes])
        normed = normed + cat([extra_ref[2 * p], extra_ref[2 * p + 1]], 0)
        out_ref[:, lanes] = normed.T.astype(out_ref.dtype)


def per_device(axes, q, k, v, e, a, f, reward, scale, shift):
    rows, columns = q.shape
    total = axes[0][1] * axes[1][1]
    owners = min(total, HEADS)
    share = HEADS // owners
    lanes = 2 * WIDTH * PAIRS
    steps = columns // lanes
    tokens = pl.BlockSpec((rows, lanes), lambda i: (0, i))
    vector = pl.BlockSpec((1, lanes), lambda i: (0, i))
    def per_head(n, m):
        return pl.BlockSpec((2 * PAIRS, n, m), lambda i: (i, 0, 0))

    maps, local, along, extra = pl.pallas_call(
        local_kernel,
        grid=(steps,),
        in_specs=[tokens] * 6 + [vector],
        out_specs=[per_head(WIDTH, 2 * WIDTH)] + [per_head(WIDTH, rows)] * 3,
        out_shape=[jax.ShapeDtypeStruct((HEADS, WIDTH, 2 * WIDTH), f32)]
        + [jax.ShapeDtypeStruct((HEADS, WIDTH, rows), f32)] * 3,
        compiler_params=pltpu.CompilerParams(vmem_limit_bytes=62 * 2**20),
        name="local",
    )(q, k, v, e, a, f, reward.reshape(1, columns))

    states = pl.pallas_call(
        functools.partial(scan_kernel, axes),
        in_specs=[pl.BlockSpec(memory_space=pltpu.VMEM)],
        out_specs=pl.BlockSpec(memory_space=pltpu.VMEM),
        out_shape=jax.ShapeDtypeStruct((HEADS, WIDTH // 2, 2 * WIDTH), f32),
        scratch_shapes=[
            pltpu.VMEM((total, share, WIDTH, 2 * WIDTH), f32),
            pltpu.VMEM((total, share, WIDTH // 2, 2 * WIDTH), f32),
            pltpu.VMEM((total, WIDTH, 2 * WIDTH), f32),
            pltpu.SemaphoreType.DMA((owners,)),
            pltpu.SemaphoreType.DMA((total,)),
            pltpu.SemaphoreType.DMA((total,)),
            pltpu.SemaphoreType.DMA((owners,)),
        ],
        compiler_params=pltpu.CompilerParams(
            collective_id=0, has_side_effects=True, vmem_limit_bytes=48 * 2**20
        ),
        name="scan",
    )(maps)

    return pl.pallas_call(
        final_kernel,
        grid=(steps,),
        in_specs=[per_head(WIDTH // 2, 2 * WIDTH)] + [per_head(WIDTH, rows)] * 3 + [vector] * 2,
        out_specs=tokens,
        out_shape=jax.ShapeDtypeStruct((rows, columns), bf16),
        compiler_params=pltpu.CompilerParams(vmem_limit_bytes=62 * 2**20),
        name="final",
    )(states, local, along, extra, scale.reshape(1, columns), shift.reshape(1, columns))


def solution(mesh):
    axes = tuple((name, mesh.shape[name]) for name in mesh.axis_names)
    placed = (P(axes_names(mesh), None),) * 6 + (P(),) * 3
    return jax.shard_map(
        functools.partial(per_device, axes),
        mesh=mesh,
        in_specs=placed,
        out_specs=P(axes_names(mesh), None),
        check_vma=False,
    )


def axes_names(mesh):
    return tuple(mesh.axis_names)
```

```python
import functools

import jax
import jax.numpy as jnp
from jax import lax
from jax.experimental import pallas as pl
from jax.experimental.pallas import tpu as pltpu
from jax.sharding import PartitionSpec as P

HEADS = 32
WIDTH = 64
PAIRS = 4
f32 = jnp.float32
bf16 = jnp.bfloat16
NN = ((1,), (0,))
NT = ((1,), (1,))
TN = ((0,), (0,))
MESH = pl.DeviceIdType.MESH


def split(x):
    hi = x.astype(bf16)
    return hi, (x - hi.astype(f32)).astype(bf16)


def dot(a, b, dims=NN):
    return lax.dot_general(a, b, (dims, ((), ())), preferred_element_type=f32)


def cat(parts, axis):
    return jnp.concatenate(parts, axis=axis)


def dot3(a, b):
    ah, al = split(a)
    bh, bl = split(b)
    n = b.shape[1]
    right = cat([cat([bh, bl], 1), cat([bh, jnp.zeros_like(bl)], 1)], 0)
    r = dot(cat([ah, al], 1), right)
    return r[:, :n] + r[:, n:]


def column(row):
    return jnp.broadcast_to(row, (8, row.shape[1])).T[:, 0:1]


def local_kernel(q_ref, k_ref, v_ref, e_ref, a_ref, f_ref, u_ref, map_ref, local_ref, along_ref, extra_ref):
    T = q_ref.shape[0]
    row = lax.broadcasted_iota(jnp.int32, (T, T), 0)
    col = lax.broadcasted_iota(jnp.int32, (T, T), 1)
    strict = row < col
    through = row <= col
    top_mask = cat([strict.astype(f32), through.astype(f32)], 1) > 0.5
    differ = row ^ col
    tri = through.astype(bf16)
    tri2 = cat([tri, tri], 0)
    eye = (row == col).astype(f32)
    heads = range(2 * PAIRS)

    kb, rt, ks, ss, vs, kb_abs, rt_abs, kt, st, last = ([] for _ in range(10))
    for p in range(PAIRS):
        lanes = slice(2 * WIDTH * p, 2 * WIDTH * (p + 1))
        q, k, v, e, a = (ref[:, lanes].astype(f32).T for ref in (q_ref, k_ref, v_ref, e_ref, a_ref))
        f = f_ref[:, lanes].T
        u = column(u_ref[:, lanes])
        fh = f.astype(bf16)
        rest = f - fh.astype(f32)
        fm = rest.astype(bf16)
        fl = (rest - fm.astype(f32)).astype(bf16)
        c = dot(cat([fh, fm], 1), tri2) + dot(fl, tri)
        end = c[:, T - 1 : T]
        mid = 0.5 * end
        e_in = jnp.exp(c - mid)
        e_before = jnp.exp(c - f - mid)
        e_inv = jnp.exp(mid - c)
        g = jnp.exp(mid)
        final = jnp.exp(end)
        qku = q * k * u
        for i in range(2):
            r = slice(WIDTH * i, WIDTH * (i + 1))
            kap = e[r] * lax.rsqrt(jnp.sum(e[r] * e[r], axis=0, keepdims=True) + 1e-06)
            stren = a[r] * kap
            kb.append(kap * e_before[r])
            rt.append(q[r] * e_in[r])
            ks.append(k[r] * e_inv[r])
            ss.append(stren * e_inv[r])
            kb_abs.append(kb[-1] * g[r])
            rt_abs.append(rt[-1] * g[r])
            kt.append(ks[-1] * g[r])
            st.append(ss[-1] * g[r])
            last.append(final[r])
            vs.append(v[r].astype(bf16))
            extra_ref[2 * p + i] = jnp.sum(qku[r], axis=0, keepdims=True) * v[r]

    mixes = []
    for h in heads:
        lh, ll = split(cat([ks[h], ss[h]], 1))
        rh, rl = split(cat([kb[h], rt[h]], 1))
        mix = cat([lh, ll], 0).T
        mixes.append(dot(cat([mix, mix], 1), cat([rh, rh, rl, rl], 0)))
    lower = [jnp.where(strict, m[T:, :T], 0.0) for m in mixes]
    read_strength = [jnp.where(through, m[T:, T:], 0.0) for m in mixes]
    values = []
    for h in heads:
        th, tl = split(jnp.where(top_mask, mixes[h][:T], 0.0))
        values.append(dot(cat([vs[h], vs[h]], 1), cat([th, tl], 0)))
    inverse = [eye - jnp.where(differ == 1, low, 0.0) for low in lower]
    bit = 1
    while (2 << bit) <= T:
        here = (differ >> bit) == 1
        step = [dot3(inverse[h], jnp.where(here, lower[h], 0.0)) for h in heads]
        inverse = [inverse[h] - dot3(step[h], inverse[h]) for h in heads]
        bit += 1
    removed = [dot3(cat([values[h][:, :T], kb_abs[h]], 0), inverse[h]) for h in heads]
    read = [dot3(removed[h], read_strength[h]) for h in heads]
    krow = lax.broadcasted_iota(jnp.int32, (WIDTH, 2 * WIDTH), 0)
    kcol = lax.broadcasted_iota(jnp.int32, (WIDTH, 2 * WIDTH), 1)
    diagonal = kcol == krow + WIDTH
    for h in heads:
        local_ref[h] = values[h][:, T:] - read[h][:WIDTH]
        along_ref[h] = rt_abs[h] - read[h][WIDTH:]
        sh, sl = split(st[h])
        kh, kl = split(kt[h])
        wh, wl = split(removed[h])
        vpad = cat([vs[h], jnp.zeros_like(vs[h])], 0)
        gain = dot(cat([kh, kl], 1), cat([vpad, vpad], 1), NT)
        loss = dot(cat([sh, sl], 1), cat([wh, wh], 1), NT) + dot(sh, wl, NT)
        map_ref[h] = gain - loss + jnp.where(diagonal, last[h], 0.0)


def slab_of(total):
    return min(8, total // 2)


def scan_kernel(
    axes, map_ref, state_ref, inbox, outbox, prefix, carry_in, carry_out, send1, recv1, send2, recv2, send3, recv3
):
    (outer_axis, outer), (inner_axis, inner) = axes
    total = outer * inner
    slab = slab_of(total)
    slabs = total // slab
    share = HEADS // slab
    me = lax.axis_index(outer_axis) * inner + lax.axis_index(inner_axis)
    z = me // slab
    base = z * slab
    pos = me - base
    half = WIDTH // 2

    def place(d):
        return (d // inner, lax.rem(d, inner))

    barrier = pltpu.get_barrier_semaphore()

    def greet(d):
        pl.semaphore_signal(barrier, inc=1, device_id=place(d), device_id_type=MESH)

    def greet_member(n, _):
        greet(base + lax.rem(pos + n, slab))
        return 0

    lax.fori_loop(1, slab, greet_member, 0)
    pl.when(z > 0)(lambda: greet(me - slab))
    pl.when(z < slabs - 1)(lambda: greet(me + slab))
    neighbours = (z + slabs - 1) // slabs + (2 * slabs - 2 - z) // slabs
    pl.semaphore_wait(barrier, slab - 1 + neighbours)

    def to_owner(j):
        return pltpu.make_async_remote_copy(
            src_ref=map_ref.at[pl.ds(j * share, share)],
            dst_ref=inbox.at[pos],
            send_sem=send1.at[j],
            recv_sem=recv1.at[pos],
            device_id=place(base + j),
            device_id_type=MESH,
        )

    def from_member(d):
        return pltpu.make_async_remote_copy(
            src_ref=map_ref.at[pl.ds(0, share)],
            dst_ref=inbox.at[d],
            send_sem=send1.at[0],
            recv_sem=recv1.at[d],
            device_id=place(base + d),
            device_id_type=MESH,
        )

    def to_member(d):
        return pltpu.make_async_remote_copy(
            src_ref=outbox.at[d],
            dst_ref=state_ref.at[pl.ds(pos * share, share)],
            send_sem=send2.at[d],
            recv_sem=recv2.at[pos],
            device_id=place(base + d),
            device_id_type=MESH,
        )

    def from_owner(j):
        return pltpu.make_async_remote_copy(
            src_ref=outbox.at[0],
            dst_ref=state_ref.at[pl.ds(j * share, share)],
            send_sem=send2.at[0],
            recv_sem=recv2.at[j],
            device_id=place(base + j),
            device_id_type=MESH,
        )

    def to_slab(d):
        return pltpu.make_async_remote_copy(
            src_ref=carry_out,
            dst_ref=carry_in,
            send_sem=send3,
            recv_sem=recv3,
            device_id=place(d),
            device_id_type=MESH,
        )

    def send_map(n, _):
        to_owner(lax.rem(pos + n, slab)).start()
        return 0

    lax.fori_loop(1, slab, send_map, 0)
    for i in range(share):
        inbox[pos, i] = map_ref[pos * share + i]

    def arrive(n, _):
        from_member(lax.rem(pos + n, slab)).wait_recv()
        return 0

    lax.fori_loop(1, slab, arrive, 0)
    krow = lax.broadcasted_iota(jnp.int32, (WIDTH, 2 * WIDTH), 0)
    kcol = lax.broadcasted_iota(jnp.int32, (WIDTH, 2 * WIDTH), 1)
    unit = (kcol == krow + WIDTH).astype(f32)
    offset = kcol < WIDTH

    def right_side(s):
        sh, sl = split(s)
        zero = jnp.zeros_like(sh)
        return cat([zero, sh, zero, sh], 0), cat([zero, sl], 0)

    def apply(m, right):
        mh, ml = split(m)
        return dot(cat([mh, ml], 1), right[0]) + dot(mh, right[1])

    def pack(s):
        return cat([s[:half], s[half:]], 1)

    def advance(t, before):
        after = []
        for i in range(share):
            prefix[t, i] = before[i]
            m = inbox[t, i]
            after.append(apply(m, right_side(before[i])) + jnp.where(offset, m, 0.0))
        return tuple(after)

    ends = lax.fori_loop(0, slab, advance, (unit,) * share)

    @pl.when(z == 0)
    def _():
        carry_in[...] = jnp.zeros_like(carry_in)

    pl.when(z > 0)(lambda: to_slab(me - slab).wait_recv())
    rights = []
    for i in range(share):
        packed = carry_in[i]
        rights.append(right_side(cat([packed[:, :WIDTH], packed[:, WIDTH:]], 0)))

    @pl.when(z < slabs - 1)
    def _():
        for i in range(share):
            carry_out[i] = pack(apply(ends[i], rights[i]) + ends[i][:, :WIDTH])
        to_slab(me + slab).start()

    def state(t, i):
        m = prefix[t, i]
        return pack(apply(m, rights[i]) + m[:, :WIDTH])

    def send_state(n, _):
        t = lax.rem(pos + n, slab)
        for i in range(share):
            outbox[t, i] = state(t, i)
        to_member(t).start()
        return 0

    lax.fori_loop(1, slab, send_state, 0)
    for i in range(share):
        state_ref[pos * share + i] = state(pos, i)

    def finish(n, _):
        j = lax.rem(pos + n, slab)
        from_owner(j).wait_recv()
        to_owner(j).wait_send()
        to_member(j).wait_send()
        return 0

    lax.fori_loop(1, slab, finish, 0)
    pl.when(z < slabs - 1)(lambda: to_slab(me + slab).wait_send())


def final_kernel(state_ref, local_ref, along_ref, extra_ref, scale_ref, shift_ref, out_ref):
    half = WIDTH // 2
    for p in range(PAIRS):
        lanes = slice(2 * WIDTH * p, 2 * WIDTH * (p + 1))
        parts = []
        for h in (2 * p, 2 * p + 1):
            packed = state_ref[h]
            s = cat([packed[:, :WIDTH], packed[:, WIDTH:]], 0)
            sh, sl = split(s)
            ah, al = split(along_ref[h])
            mixed = local_ref[h] + dot(cat([sh, sh, sl], 0), cat([ah, al, ah], 0), TN)
            center = mixed - jnp.mean(mixed, axis=0, keepdims=True)
            variance = jnp.mean(center * center, axis=0, keepdims=True)
            parts.append(center * lax.rsqrt(variance + 0.00064))
        normed = cat(parts, 0) * column(scale_ref[:, lanes]) + column(shift_ref[:, lanes])
        normed = normed + cat([extra_ref[2 * p], extra_ref[2 * p + 1]], 0)
        out_ref[:, lanes] = normed.T.astype(out_ref.dtype)


def per_device(axes, q, k, v, e, a, f, reward, scale, shift):
    rows, columns = q.shape
    total = axes[0][1] * axes[1][1]
    slab = slab_of(total)
    share = HEADS // slab
    lanes = 2 * WIDTH * PAIRS
    steps = columns // lanes
    tokens = pl.BlockSpec((rows, lanes), lambda i: (0, i))
    vector = pl.BlockSpec((1, lanes), lambda i: (0, i))
    def per_head(n, m):
        return pl.BlockSpec((2 * PAIRS, n, m), lambda i: (i, 0, 0))

    maps, local, along, extra = pl.pallas_call(
        local_kernel,
        grid=(steps,),
        in_specs=[tokens] * 6 + [vector],
        out_specs=[per_head(WIDTH, 2 * WIDTH)] + [per_head(WIDTH, rows)] * 3,
        out_shape=[jax.ShapeDtypeStruct((HEADS, WIDTH, 2 * WIDTH), f32)]
        + [jax.ShapeDtypeStruct((HEADS, WIDTH, rows), f32)] * 3,
        compiler_params=pltpu.CompilerParams(vmem_limit_bytes=62 * 2**20),
        name="local",
    )(q, k, v, e, a, f, reward.reshape(1, columns))

    states = pl.pallas_call(
        functools.partial(scan_kernel, axes),
        in_specs=[pl.BlockSpec(memory_space=pltpu.VMEM)],
        out_specs=pl.BlockSpec(memory_space=pltpu.VMEM),
        out_shape=jax.ShapeDtypeStruct((HEADS, WIDTH // 2, 2 * WIDTH), f32),
        scratch_shapes=[
            pltpu.VMEM((slab, share, WIDTH, 2 * WIDTH), f32),
            pltpu.VMEM((slab, share, WIDTH // 2, 2 * WIDTH), f32),
            pltpu.VMEM((slab, share, WIDTH, 2 * WIDTH), f32),
            pltpu.VMEM((share, WIDTH // 2, 2 * WIDTH), f32),
            pltpu.VMEM((share, WIDTH // 2, 2 * WIDTH), f32),
        ]
        + [pltpu.SemaphoreType.DMA((slab,))] * 4
        + [pltpu.SemaphoreType.DMA] * 2,
        compiler_params=pltpu.CompilerParams(
            collective_id=0, has_side_effects=True, vmem_limit_bytes=48 * 2**20
        ),
        name="scan",
    )(maps)

    return pl.pallas_call(
        final_kernel,
        grid=(steps,),
        in_specs=[per_head(WIDTH // 2, 2 * WIDTH)] + [per_head(WIDTH, rows)] * 3 + [vector] * 2,
        out_specs=tokens,
        out_shape=jax.ShapeDtypeStruct((rows, columns), bf16),
        compiler_params=pltpu.CompilerParams(vmem_limit_bytes=62 * 2**20),
        name="final",
    )(states, local, along, extra, scale.reshape(1, columns), shift.reshape(1, columns))


def solution(mesh):
    axes = tuple((name, mesh.shape[name]) for name in mesh.axis_names)
    placed = (P(axes_names(mesh), None),) * 6 + (P(),) * 3
    return jax.shard_map(
        functools.partial(per_device, axes),
        mesh=mesh,
        in_specs=placed,
        out_specs=P(axes_names(mesh), None),
        check_vma=False,
    )


def axes_names(mesh):
    return tuple(mesh.axis_names)
```

```python
import functools

import jax
import jax.numpy as jnp
from jax import lax
from jax.experimental import pallas as pl
from jax.experimental.pallas import tpu as pltpu
from jax.sharding import PartitionSpec as P

HEADS = 32
WIDTH = 64
PAIRS = 8
f32 = jnp.float32
bf16 = jnp.bfloat16
NN = ((1,), (0,))
NT = ((1,), (1,))
TN = ((0,), (0,))
MESH = pl.DeviceIdType.MESH


def split(x):
    hi = x.astype(bf16)
    return hi, (x - hi.astype(f32)).astype(bf16)


def dot(a, b, dims=NN):
    return lax.dot_general(a, b, (dims, ((), ())), preferred_element_type=f32)


def cat(parts, axis):
    return jnp.concatenate(parts, axis=axis)


def dot3(a, b):
    ah, al = split(a)
    bh, bl = split(b)
    n = b.shape[1]
    right = cat([cat([bh, bl], 1), cat([bh, jnp.zeros_like(bl)], 1)], 0)
    r = dot(cat([ah, al], 1), right)
    return r[:, :n] + r[:, n:]


def column(row):
    return jnp.broadcast_to(row, (8, row.shape[1])).T[:, 0:1]


def local_kernel(q_ref, k_ref, v_ref, e_ref, a_ref, f_ref, u_ref, map_ref, local_ref, along_ref, extra_ref):
    T = q_ref.shape[0]
    row = lax.broadcasted_iota(jnp.int32, (T, T), 0)
    col = lax.broadcasted_iota(jnp.int32, (T, T), 1)
    strict = row < col
    through = row <= col
    top_mask = cat([strict.astype(f32), through.astype(f32)], 1) > 0.5
    differ = row ^ col
    tri = through.astype(bf16)
    tri2 = cat([tri, tri], 0)
    eye = (row == col).astype(f32)
    heads = range(2 * PAIRS)

    kb, rt, ks, ss, vs, kb_abs, rt_abs, kt, st, last = ([] for _ in range(10))
    for p in range(PAIRS):
        lanes = slice(2 * WIDTH * p, 2 * WIDTH * (p + 1))
        q, k, v, e, a = (ref[:, lanes].astype(f32).T for ref in (q_ref, k_ref, v_ref, e_ref, a_ref))
        f = f_ref[:, lanes].T
        u = column(u_ref[:, lanes])
        fh = f.astype(bf16)
        rest = f - fh.astype(f32)
        fm = rest.astype(bf16)
        fl = (rest - fm.astype(f32)).astype(bf16)
        c = dot(cat([fh, fm], 1), tri2) + dot(fl, tri)
        end = c[:, T - 1 : T]
        mid = 0.5 * end
        e_in = jnp.exp(c - mid)
        e_before = jnp.exp(c - f - mid)
        e_inv = jnp.exp(mid - c)
        g = jnp.exp(mid)
        final = jnp.exp(end)
        qku = q * k * u
        for i in range(2):
            r = slice(WIDTH * i, WIDTH * (i + 1))
            kap = e[r] * lax.rsqrt(jnp.sum(e[r] * e[r], axis=0, keepdims=True) + 1e-06)
            stren = a[r] * kap
            kb.append(kap * e_before[r])
            rt.append(q[r] * e_in[r])
            ks.append(k[r] * e_inv[r])
            ss.append(stren * e_inv[r])
            kb_abs.append(kb[-1] * g[r])
            rt_abs.append(rt[-1] * g[r])
            kt.append(ks[-1] * g[r])
            st.append(ss[-1] * g[r])
            last.append(final[r])
            vs.append(v[r].astype(bf16))
            extra_ref[2 * p + i] = jnp.sum(qku[r], axis=0, keepdims=True) * v[r]

    mixes = []
    for h in heads:
        lh, ll = split(cat([ks[h], ss[h]], 1))
        rh, rl = split(cat([kb[h], rt[h]], 1))
        mix = cat([lh, ll], 0).T
        mixes.append(dot(cat([mix, mix], 1), cat([rh, rh, rl, rl], 0)))
    lower = [jnp.where(strict, m[T:, :T], 0.0) for m in mixes]
    read_strength = [jnp.where(through, m[T:, T:], 0.0) for m in mixes]
    values = []
    for h in heads:
        th, tl = split(jnp.where(top_mask, mixes[h][:T], 0.0))
        values.append(dot(cat([vs[h], vs[h]], 1), cat([th, tl], 0)))
    inverse = [eye - jnp.where(differ == 1, low, 0.0) for low in lower]
    bit = 1
    while (2 << bit) <= T:
        here = (differ >> bit) == 1
        step = [dot3(inverse[h], jnp.where(here, lower[h], 0.0)) for h in heads]
        inverse = [inverse[h] - dot3(step[h], inverse[h]) for h in heads]
        bit += 1
    removed = [dot3(cat([values[h][:, :T], kb_abs[h]], 0), inverse[h]) for h in heads]
    read = [dot3(removed[h], read_strength[h]) for h in heads]
    krow = lax.broadcasted_iota(jnp.int32, (WIDTH, 2 * WIDTH), 0)
    kcol = lax.broadcasted_iota(jnp.int32, (WIDTH, 2 * WIDTH), 1)
    diagonal = kcol == krow + WIDTH
    for h in heads:
        local_ref[h] = values[h][:, T:] - read[h][:WIDTH]
        along_ref[h] = rt_abs[h] - read[h][WIDTH:]
        sh, sl = split(st[h])
        kh, kl = split(kt[h])
        wh, wl = split(removed[h])
        vpad = cat([vs[h], jnp.zeros_like(vs[h])], 0)
        gain = dot(cat([kh, kl], 1), cat([vpad, vpad], 1), NT)
        loss = dot(cat([sh, sl], 1), cat([wh, wh], 1), NT) + dot(sh, wl, NT)
        map_ref[h] = gain - loss + jnp.where(diagonal, last[h], 0.0)


def slab_of(total):
    return min(8, total // 2)


def scan_kernel(
    axes, map_ref, state_ref, inbox, outbox, prefix, carry_in, carry_out, send1, recv1, send2, recv2, send3, recv3
):
    (outer_axis, outer), (inner_axis, inner) = axes
    total = outer * inner
    slab = slab_of(total)
    slabs = total // slab
    share = HEADS // slab
    me = lax.axis_index(outer_axis) * inner + lax.axis_index(inner_axis)
    z = me // slab
    base = z * slab
    pos = me - base
    half = WIDTH // 2

    def place(d):
        return (d // inner, lax.rem(d, inner))

    barrier = pltpu.get_barrier_semaphore()

    def greet(d):
        pl.semaphore_signal(barrier, inc=1, device_id=place(d), device_id_type=MESH)

    def greet_member(n, _):
        greet(base + lax.rem(pos + n, slab))
        return 0

    lax.fori_loop(1, slab, greet_member, 0)
    pl.when(z > 0)(lambda: greet(me - slab))
    pl.when(z < slabs - 1)(lambda: greet(me + slab))
    neighbours = (z + slabs - 1) // slabs + (2 * slabs - 2 - z) // slabs
    pl.semaphore_wait(barrier, slab - 1 + neighbours)

    def to_owner(j):
        return pltpu.make_async_remote_copy(
            src_ref=map_ref.at[pl.ds(j * share, share)],
            dst_ref=inbox.at[pos],
            send_sem=send1.at[j],
            recv_sem=recv1.at[pos],
            device_id=place(base + j),
            device_id_type=MESH,
        )

    def from_member(d):
        return pltpu.make_async_remote_copy(
            src_ref=map_ref.at[pl.ds(0, share)],
            dst_ref=inbox.at[d],
            send_sem=send1.at[0],
            recv_sem=recv1.at[d],
            device_id=place(base + d),
            device_id_type=MESH,
        )

    def to_member(d):
        return pltpu.make_async_remote_copy(
            src_ref=outbox.at[d],
            dst_ref=state_ref.at[pl.ds(pos * share, share)],
            send_sem=send2.at[d],
            recv_sem=recv2.at[pos],
            device_id=place(base + d),
            device_id_type=MESH,
        )

    def from_owner(j):
        return pltpu.make_async_remote_copy(
            src_ref=outbox.at[0],
            dst_ref=state_ref.at[pl.ds(j * share, share)],
            send_sem=send2.at[0],
            recv_sem=recv2.at[j],
            device_id=place(base + j),
            device_id_type=MESH,
        )

    def to_slab(d):
        return pltpu.make_async_remote_copy(
            src_ref=carry_out,
            dst_ref=carry_in,
            send_sem=send3,
            recv_sem=recv3,
            device_id=place(d),
            device_id_type=MESH,
        )

    def send_map(n, _):
        to_owner(lax.rem(pos + n, slab)).start()
        return 0

    lax.fori_loop(1, slab, send_map, 0)
    for i in range(share):
        inbox[pos, i] = map_ref[pos * share + i]

    def arrive(n, _):
        from_member(lax.rem(pos + n, slab)).wait_recv()
        return 0

    lax.fori_loop(1, slab, arrive, 0)
    krow = lax.broadcasted_iota(jnp.int32, (WIDTH, 2 * WIDTH), 0)
    kcol = lax.broadcasted_iota(jnp.int32, (WIDTH, 2 * WIDTH), 1)
    unit = (kcol == krow + WIDTH).astype(f32)
    offset = kcol < WIDTH

    def right_side(s):
        sh, sl = split(s)
        zero = jnp.zeros_like(sh)
        return cat([zero, sh, zero, sh], 0), cat([zero, sl], 0)

    def apply(m, right):
        mh, ml = split(m)
        return dot(cat([mh, ml], 1), right[0]) + dot(mh, right[1])

    def pack(s):
        return cat([s[:half], s[half:]], 1)

    def advance(t, before):
        after = []
        for i in range(share):
            prefix[t, i] = before[i]
            m = inbox[t, i]
            after.append(apply(m, right_side(before[i])) + jnp.where(offset, m, 0.0))
        return tuple(after)

    ends = lax.fori_loop(0, slab, advance, (unit,) * share)

    @pl.when(z == 0)
    def _():
        carry_in[...] = jnp.zeros_like(carry_in)

    pl.when(z > 0)(lambda: to_slab(me - slab).wait_recv())
    rights = []
    for i in range(share):
        packed = carry_in[i]
        rights.append(right_side(cat([packed[:, :WIDTH], packed[:, WIDTH:]], 0)))

    @pl.when(z < slabs - 1)
    def _():
        for i in range(share):
            carry_out[i] = pack(apply(ends[i], rights[i]) + ends[i][:, :WIDTH])
        to_slab(me + slab).start()

    def state(t, i):
        m = prefix[t, i]
        return pack(apply(m, rights[i]) + m[:, :WIDTH])

    def send_state(n, _):
        t = lax.rem(pos + n, slab)
        for i in range(share):
            outbox[t, i] = state(t, i)
        to_member(t).start()
        return 0

    lax.fori_loop(1, slab, send_state, 0)
    for i in range(share):
        state_ref[pos * share + i] = state(pos, i)

    def finish(n, _):
        j = lax.rem(pos + n, slab)
        from_owner(j).wait_recv()
        to_owner(j).wait_send()
        to_member(j).wait_send()
        return 0

    lax.fori_loop(1, slab, finish, 0)
    pl.when(z < slabs - 1)(lambda: to_slab(me + slab).wait_send())


def final_kernel(state_ref, local_ref, along_ref, extra_ref, scale_ref, shift_ref, out_ref):
    half = WIDTH // 2
    for p in range(PAIRS):
        lanes = slice(2 * WIDTH * p, 2 * WIDTH * (p + 1))
        parts = []
        for h in (2 * p, 2 * p + 1):
            packed = state_ref[h]
            s = cat([packed[:, :WIDTH], packed[:, WIDTH:]], 0)
            sh, sl = split(s)
            ah, al = split(along_ref[h])
            mixed = local_ref[h] + dot(cat([sh, sh, sl], 0), cat([ah, al, ah], 0), TN)
            center = mixed - jnp.mean(mixed, axis=0, keepdims=True)
            variance = jnp.mean(center * center, axis=0, keepdims=True)
            parts.append(center * lax.rsqrt(variance + 0.00064))
        normed = cat(parts, 0) * column(scale_ref[:, lanes]) + column(shift_ref[:, lanes])
        normed = normed + cat([extra_ref[2 * p], extra_ref[2 * p + 1]], 0)
        out_ref[:, lanes] = normed.T.astype(out_ref.dtype)


def per_device(axes, q, k, v, e, a, f, reward, scale, shift):
    rows, columns = q.shape
    total = axes[0][1] * axes[1][1]
    slab = slab_of(total)
    share = HEADS // slab
    lanes = 2 * WIDTH * PAIRS
    steps = columns // lanes
    tokens = pl.BlockSpec((rows, lanes), lambda i: (0, i))
    vector = pl.BlockSpec((1, lanes), lambda i: (0, i))
    def per_head(n, m):
        return pl.BlockSpec((2 * PAIRS, n, m), lambda i: (i, 0, 0))

    maps, local, along, extra = pl.pallas_call(
        local_kernel,
        grid=(steps,),
        in_specs=[tokens] * 6 + [vector],
        out_specs=[per_head(WIDTH, 2 * WIDTH)] + [per_head(WIDTH, rows)] * 3,
        out_shape=[jax.ShapeDtypeStruct((HEADS, WIDTH, 2 * WIDTH), f32)]
        + [jax.ShapeDtypeStruct((HEADS, WIDTH, rows), f32)] * 3,
        compiler_params=pltpu.CompilerParams(vmem_limit_bytes=62 * 2**20),
        name="local",
    )(q, k, v, e, a, f, reward.reshape(1, columns))

    states = pl.pallas_call(
        functools.partial(scan_kernel, axes),
        in_specs=[pl.BlockSpec(memory_space=pltpu.VMEM)],
        out_specs=pl.BlockSpec(memory_space=pltpu.VMEM),
        out_shape=jax.ShapeDtypeStruct((HEADS, WIDTH // 2, 2 * WIDTH), f32),
        scratch_shapes=[
            pltpu.VMEM((slab, share, WIDTH, 2 * WIDTH), f32),
            pltpu.VMEM((slab, share, WIDTH // 2, 2 * WIDTH), f32),
            pltpu.VMEM((slab, share, WIDTH, 2 * WIDTH), f32),
            pltpu.VMEM((share, WIDTH // 2, 2 * WIDTH), f32),
            pltpu.VMEM((share, WIDTH // 2, 2 * WIDTH), f32),
        ]
        + [pltpu.SemaphoreType.DMA((slab,))] * 4
        + [pltpu.SemaphoreType.DMA] * 2,
        compiler_params=pltpu.CompilerParams(
            collective_id=0, has_side_effects=True, vmem_limit_bytes=48 * 2**20
        ),
        name="scan",
    )(maps)

    return pl.pallas_call(
        final_kernel,
        grid=(steps,),
        in_specs=[per_head(WIDTH // 2, 2 * WIDTH)] + [per_head(WIDTH, rows)] * 3 + [vector] * 2,
        out_specs=tokens,
        out_shape=jax.ShapeDtypeStruct((rows, columns), bf16),
        compiler_params=pltpu.CompilerParams(vmem_limit_bytes=62 * 2**20),
        name="final",
    )(states, local, along, extra, scale.reshape(1, columns), shift.reshape(1, columns))


def solution(mesh):
    axes = tuple((name, mesh.shape[name]) for name in mesh.axis_names)
    placed = (P(axes_names(mesh), None),) * 6 + (P(),) * 3
    return jax.shard_map(
        functools.partial(per_device, axes),
        mesh=mesh,
        in_specs=placed,
        out_specs=P(axes_names(mesh), None),
        check_vma=False,
    )


def axes_names(mesh):
    return tuple(mesh.axis_names)
```
